256 devices in a mesh: row: 8 (over z_lo, core), col: 32 (over x, y, z_hi).
Axes of the slice: x: 4, y: 4, z: 8 (z_hi: 2, z_lo: 4; z = z_hi * 4 + z_lo), core: 2. Of those that a mesh axis runs over, the one named last changes fastest.
Arguments:
- mat_a: bfloat16 [20480, 49152], P('row', 'col'), may hold values from -6 to 6
- mat_b: bfloat16 [49152, 8192], P('row', 'col'), may hold values from -0.15625 to 0.15625
- mask_a: int32 [160, 384], P('row', 'col'), may hold values from 0 to 1, as said below
- mask_b: int32 [384, 64], P('row', 'col'), may hold values 0 or 1
Outputs:
- product: bfloat16 [20480, 8192], P('row', 'col')
The draws below stay inside these ranges and needn't reach their ends.
Inputs may be any that keep to these rules, and one draw needn't show every extreme that they name: `mask_a`: in each tile of 20 x 12 entries, the block rows holding an occupied block come first and each holds at least one; in every draw some tile has all 20 block rows occupied.
All inputs are finite; a program needn't handle non-finite values. No bound on the sum of `mask_b` on one device may be relied on, other than what follows from the above.
Results may differ from the reference program's by a relative error of at most 0.0025.
Values may be sent and summed in bfloat16 or wider, within the bound.
No kernel may reach another device: no remote copies, remote signals or barrier semaphores. Data moves between devices by JAX's collectives and lax.ppermute only.
A program may use at most 128 MiB of HBM per device.

```python
import jax
import jax.numpy as jnp
from jax import lax

BLK = 128
RB = 20
KB = 12
CB = 2
SLOTS = 4
ROWS = 20480
INNER = 49152
COLS = 8192
N_ROW = 8
N_COL = 32


def draw_mask_a(key, part):
    keys = jax.random.split(jax.random.fold_in(key, 11), 5)
    heavy = jax.random.randint(keys[0], (N_ROW, N_COL), 0, 4) == 0
    light = jax.random.randint(keys[1], (N_ROW, N_COL), 1, min(4, RB) + 1)
    counts = jnp.where(heavy, RB, light)
    chosen = jax.random.randint(keys[2], (), 0, N_ROW * N_COL)
    places = jnp.arange(N_ROW * N_COL).reshape(N_ROW, N_COL)
    counts = jnp.where(places == chosen, RB, counts)
    blocks = jax.random.randint(keys[3], (N_ROW, RB, N_COL, KB), 0, 4) != 0
    needed = jax.random.randint(keys[4], (N_ROW, RB, N_COL, 1), 0, KB)
    blocks = jnp.logical_or(blocks, jnp.arange(KB)[None, None, None, :] == needed)
    living = jnp.arange(RB)[None, :, None, None] < counts[:, None, :, None]
    occupied = jnp.logical_and(blocks, living).astype(jnp.int32)
    return occupied.reshape(N_ROW * RB, N_COL * KB)


def touch_ends(drawn, own_key, smallest, high):
    longest = drawn.shape.index(max(drawn.shape))
    spots = []
    for shift in (0, 1):
        where = [jax.random.randint(jax.random.fold_in(own_key, axis), (), 0, length) for axis, length in enumerate(drawn.shape)]
        where[longest] = (where[longest] + shift) % drawn.shape[longest]
        spots.append(tuple(where))
    return drawn.at[spots[0]].set(smallest).at[spots[1]].set(high)


def steps_of(stream_key, shape, cuts, smallest, largest):
    def one(position, shards_of):
        heights = jax.random.uniform(jax.random.fold_in(jax.random.fold_in(stream_key, 6), position), (shards_of,), jnp.float32, smallest / len(cuts), largest / len(cuts))
        return jnp.repeat(jnp.exp(heights), shape[position] // shards_of).reshape((-1,) + (1,) * (len(shape) - position - 1))

    loudness = one(*cuts[0])
    for cut in cuts[1:]:
        loudness = loudness * one(*cut)
    return loudness


def gaussian(key, extent, scale, most, cuts=(), held_as=jnp.bfloat16):
    gain = steps_of(key, extent, cuts, -0.22, 0.18) if cuts else 1.0
    drawn = jax.random.normal(key, extent, jnp.float32) * scale * gain
    return jnp.minimum(jnp.maximum(drawn, -most), most).astype(held_as)


def setup_inputs(seed: int = 0) -> dict:
    splits = jax.random.split(jax.random.key(seed), 5)
    return {
        "mat_a": gaussian(splits[0], (ROWS, INNER), 1.0, 6.0, ((0, 8), (1, 32))),
        "mat_b": gaussian(splits[1], (INNER, COLS), (KB * BLK) ** -0.5, 0.15625, ((0, 8), (1, 32))),
        "mask_a": draw_mask_a(jax.random.fold_in(splits[4], 71), 0),
        "mask_b": touch_ends((jax.random.randint(splits[3], (N_COL * KB, N_COL * CB), 0, 4) < 3).astype(jnp.int32), jax.random.fold_in(splits[3], 1), 0, 1),
    }


def mask_blocks(matrix, occupied):
    rows, columns = occupied.shape
    blocked = matrix.reshape(rows, matrix.shape[0] // rows, columns, matrix.shape[1] // columns)
    scaling = occupied.astype(matrix.dtype)[:, None, :, None]
    return (blocked * scaling).reshape(matrix.shape)


def row_product(matrix_rows, right_tile, live_flags):
    stacked = matrix_rows.reshape(RB, BLK, matrix_rows.shape[1])

    def one_row(inputs):
        row_block, flagged = inputs
        return lax.cond(
            flagged,
            lambda piece: jnp.dot(piece, right_tile, preferred_element_type=jnp.float32),
            lambda piece: jnp.zeros((BLK, right_tile.shape[1]), jnp.float32),
            row_block,
        )

    return lax.map(one_row, (stacked, live_flags)).reshape(RB * BLK, right_tile.shape[1])


def reference(mat_a, mat_b, mask_a, mask_b):
    masked_a = mask_blocks(mat_a, mask_a)
    masked_b = mask_blocks(mat_b, mask_b)
    tiles_a = masked_a.reshape(N_ROW, RB * BLK, N_COL, KB * BLK).transpose(0, 2, 1, 3)
    stacked = masked_b.reshape(N_ROW, SLOTS, KB * BLK, N_COL, CB * BLK).transpose(0, 3, 1, 2, 4)
    first_b = stacked[:, :, 0]
    sent_b = jnp.concatenate([stacked[:1, :, 1], stacked[1:, :, 0]], axis=0)
    next_b = jnp.roll(sent_b, -1, axis=0)
    live_a = jnp.any(mask_a.reshape(N_ROW, RB, N_COL, KB) > 0, axis=3).transpose(0, 2, 1)
    next_a = jnp.roll(tiles_a, -1, axis=1)
    next_live = jnp.roll(live_a, -1, axis=1)
    count = N_ROW * N_COL
    inputs = (
        tiles_a.reshape(count, RB * BLK, KB * BLK),
        first_b.reshape(count, KB * BLK, CB * BLK),
        live_a.reshape(count, RB),
        next_a.reshape(count, RB * BLK, KB * BLK),
        next_b.reshape(count, KB * BLK, CB * BLK),
        next_live.reshape(count, RB),
    )

    def one_tile(pieces):
        first_a, first_right, first_live, second_a, second_right, second_live = pieces
        summed = row_product(first_a, first_right, first_live) + row_product(second_a, second_right, second_live)
        return summed.astype(jnp.bfloat16)

    result = lax.map(one_tile, inputs)
    result = result.reshape(N_ROW, N_COL, RB * BLK, CB * BLK).transpose(0, 2, 1, 3)
    return result.reshape(N_ROW * RB * BLK, N_COL * CB * BLK)
```

```python
import functools

import jax
import jax.numpy as jnp
from jax import lax
from jax.experimental import pallas as pl
from jax.experimental.pallas import tpu as pltpu
from jax.sharding import PartitionSpec as P

BLK = 128
STEP_BLOCKS = 5
PAD = 16
HALVES = 2
VMEM = 60 * 1024 * 1024


def masked(block, flag):
    return jnp.where(flag > 0, block, jnp.zeros_like(block))


def pick_kernel(slot_ref, mask_ref, b_ref, out_ref, *, blocks):
    base = slot_ref[0] * blocks
    for k in range(blocks):
        for c in range(out_ref.shape[1] // BLK):
            rows, cols = pl.ds(k * BLK, BLK), pl.ds(c * BLK, BLK)
            out_ref[rows, cols] = masked(b_ref[rows, cols], mask_ref[base + k, c])


def pick_b(mat_b, mask_b, slot, depth):
    columns = mat_b.shape[1]
    return pl.pallas_call(
        functools.partial(pick_kernel, blocks=depth // BLK),
        grid_spec=pltpu.PrefetchScalarGridSpec(
            num_scalar_prefetch=2,
            grid=(1,),
            in_specs=[pl.BlockSpec((depth, columns), lambda g, slot, mask: (slot[0], 0))],
            out_specs=pl.BlockSpec((depth, columns), lambda g, slot, mask: (0, 0)),
        ),
        out_shape=jax.ShapeDtypeStruct((depth, columns), mat_b.dtype),
        compiler_params=pltpu.CompilerParams(vmem_limit_bytes=VMEM),
        name="pick_b",
    )(slot, mask_b, mat_b)


def mask_rows(mask_ref, a_ref, held, first_block):
    for r in range(a_ref.shape[0] // BLK):
        for k in range(a_ref.shape[1] // BLK):
            rows, cols = pl.ds(r * BLK, BLK), pl.ds(k * BLK, BLK)
            held[rows, cols] = masked(a_ref[rows, cols], mask_ref[first_block + r, k])


def own_kernel(mask_a_ref, mask_b_ref, a_ref, b_ref, out_ref, held_a, held_b):
    step = pl.program_id(0)

    @pl.when(step == 0)
    def _():
        for k in range(b_ref.shape[0] // BLK):
            for c in range(b_ref.shape[1] // BLK):
                rows, cols = pl.ds(k * BLK, BLK), pl.ds(c * BLK, BLK)
                held_b[rows, cols] = masked(b_ref[rows, cols], mask_b_ref[k, c])

    mask_rows(mask_a_ref, a_ref, held_a, step * STEP_BLOCKS)
    out_ref[...] = jnp.dot(held_a[...], held_b[...], preferred_element_type=jnp.float32)


def own_product(mat_a, mat_b, mask_a, mask_b):
    rows, depth = mat_a.shape
    columns = mat_b.shape[1]
    height = STEP_BLOCKS * BLK
    return pl.pallas_call(
        own_kernel,
        grid_spec=pltpu.PrefetchScalarGridSpec(
            num_scalar_prefetch=2,
            grid=(rows // height,),
            in_specs=[
                pl.BlockSpec((height, depth), lambda g, ma, mb: (g, 0)),
                pl.BlockSpec((depth, columns), lambda g, ma, mb: (0, 0)),
            ],
            out_specs=pl.BlockSpec((height, columns), lambda g, ma, mb: (g, 0)),
            scratch_shapes=[
                pltpu.VMEM((height, depth), mat_a.dtype),
                pltpu.VMEM((depth, columns), mat_b.dtype),
            ],
        ),
        out_shape=jax.ShapeDtypeStruct((rows, columns), jnp.float32),
        compiler_params=pltpu.CompilerParams(vmem_limit_bytes=VMEM),
        cost_estimate=pl.CostEstimate(
            flops=2 * rows * depth * columns, bytes_accessed=2 * rows * depth + 4 * rows * columns, transcendentals=0
        ),
        name="own_product",
    )(mask_a, mask_b, mat_a, mat_b)


def away_kernel(mask_a_ref, a_ref, b_ref, out_ref, held_a, *, first):
    step = pl.program_id(0)
    mask_rows(mask_a_ref, a_ref, held_a, (first + step) * STEP_BLOCKS)
    product = jnp.dot(held_a[...], b_ref[...], preferred_element_type=jnp.float32)
    place = lax.broadcasted_iota(jnp.int32, (PAD, product.shape[1]), 0)
    powers = jnp.zeros(place.shape, jnp.float32)
    for r in range(STEP_BLOCKS):
        piece = product[r * BLK : (r + 1) * BLK]
        most = jnp.max(jnp.max(jnp.abs(piece), axis=0, keepdims=True), axis=1, keepdims=True)
        power = jnp.ceil(jnp.log2(jnp.maximum(most, 1e-30)) + 0.01)
        coded = jnp.round(piece * (32767.0 * jnp.exp2(-power)))
        coded = jnp.clip(coded, -32767.0, 32767.0)
        out_ref[r * BLK : (r + 1) * BLK] = coded.astype(jnp.int32).astype(jnp.int16)
        powers = jnp.where(place == r, power, powers)
    out_ref[STEP_BLOCKS * BLK :] = powers.astype(jnp.int32).astype(jnp.int16)


def away_product(mat_a, right, mask_a, first, steps):
    depth = mat_a.shape[1]
    columns = right.shape[1]
    height = STEP_BLOCKS * BLK
    return pl.pallas_call(
        functools.partial(away_kernel, first=first),
        grid_spec=pltpu.PrefetchScalarGridSpec(
            num_scalar_prefetch=1,
            grid=(steps,),
            in_specs=[
                pl.BlockSpec((height, depth), lambda g, ma: (first + g, 0)),
                pl.BlockSpec((depth, columns), lambda g, ma: (0, 0)),
            ],
            out_specs=pl.BlockSpec((height + PAD, columns), lambda g, ma: (g, 0)),
            scratch_shapes=[pltpu.VMEM((height, depth), mat_a.dtype)],
        ),
        out_shape=jax.ShapeDtypeStruct((steps * (height + PAD), columns), jnp.int16),
        compiler_params=pltpu.CompilerParams(vmem_limit_bytes=VMEM),
        cost_estimate=pl.CostEstimate(
            flops=2 * steps * height * depth * columns, bytes_accessed=2 * steps * height * depth, transcendentals=0
        ),
        name="away_product",
    )(mask_a, mat_a, right)


def join_kernel(first_ref, coded_ref, *rest):
    out_ref = rest[-1]
    powers = coded_ref[STEP_BLOCKS * BLK :].astype(jnp.int32).astype(jnp.float32)
    for r in range(STEP_BLOCKS):
        rows = slice(r * BLK, (r + 1) * BLK)
        scale = jnp.exp2(powers[r : r + 1]) * (1.0 / 32767.0)
        far = coded_ref[rows].astype(jnp.int32).astype(jnp.float32) * scale
        out_ref[rows] = (first_ref[rows] + far).astype(jnp.bfloat16)


def join(own, coded, held, first, steps):
    rows, columns = own.shape
    height = STEP_BLOCKS * BLK
    specs = [
        pl.BlockSpec((height, columns), lambda g: (first + g, 0)),
        pl.BlockSpec((height + PAD, columns), lambda g: (g, 0)),
    ]
    operands = [own, coded]
    aliases = {}
    if held is not None:
        specs.append(pl.BlockSpec(memory_space=pl.ANY))
        operands.append(held)
        aliases = {2: 0}
    return pl.pallas_call(
        join_kernel,
        grid=(steps,),
        in_specs=specs,
        out_specs=pl.BlockSpec((height, columns), lambda g: (first + g, 0)),
        out_shape=jax.ShapeDtypeStruct((rows, columns), jnp.bfloat16),
        input_output_aliases=aliases,
        compiler_params=pltpu.CompilerParams(vmem_limit_bytes=VMEM),
        cost_estimate=pl.CostEstimate(
            flops=2 * steps * height * columns, bytes_accessed=8 * steps * height * columns, transcendentals=0
        ),
        name="join",
    )(*operands)


def body(mat_a, mat_b, mask_a, mask_b):
    depth = mat_a.shape[1]
    n_row, n_col = lax.axis_size("row"), lax.axis_size("col")
    slot = jnp.where(lax.axis_index("row") == 0, 1, 0).astype(jnp.int32)[None]
    give_b = [
        (i * n_col + j, ((i - 1) % n_row) * n_col + (j + 1) % n_col) for i in range(n_row) for j in range(n_col)
    ]
    give_c = [(i * n_col + j, i * n_col + (j - 1) % n_col) for i in range(n_row) for j in range(n_col)]
    right = lax.ppermute(pick_b(mat_b, mask_b, slot, depth), ("row", "col"), give_b)
    own = own_product(mat_a, mat_b, mask_a, mask_b)
    steps = mat_a.shape[0] // (STEP_BLOCKS * BLK) // HALVES
    arrived = []
    for half in range(HALVES):
        coded = away_product(mat_a, right, mask_a, half * steps, steps)
        arrived.append(lax.ppermute(coded, ("row", "col"), give_c))
    out = None
    for half in range(HALVES):
        out = join(own, arrived[half], out, half * steps, steps)
    return out


def solution(mesh):
    return jax.shard_map(
        body,
        mesh=mesh,
        in_specs=(P("row", "col"), P("row", "col"), P("row", "col"), P("row", "col")),
        out_specs=P("row", "col"),
        check_vma=False,
    )
```

```python
import functools

import jax
import jax.numpy as jnp
from jax import lax
from jax.experimental import pallas as pl
from jax.experimental.pallas import tpu as pltpu
from jax.sharding import PartitionSpec as P

BLK = 128
STEP_BLOCKS = 5
PAD = 16
JOIN_BLOCKS = 5
PARTS = 2
MIB = 1024 * 1024


def masked(block, flag):
    return jnp.where(flag > 0, block, jnp.zeros_like(block))


def pick_kernel(place_ref, mask_ref, *refs):
    for which in range(2):
        b_ref, out_ref = refs[which], refs[2 + which]
        blocks = b_ref.shape[0] // BLK
        base = place_ref[which] * blocks
        for k in range(blocks):
            for c in range(b_ref.shape[1] // BLK):
                rows, cols = pl.ds(k * BLK, BLK), pl.ds(c * BLK, BLK)
                out_ref[rows, cols] = masked(b_ref[rows, cols], mask_ref[c, base + k])


def pick_b(mat_b, mask_b, places, half):
    columns = mat_b.shape[1]
    return pl.pallas_call(
        pick_kernel,
        grid_spec=pltpu.PrefetchScalarGridSpec(
            num_scalar_prefetch=2,
            grid=(1,),
            in_specs=[
                pl.BlockSpec((half, columns), lambda g, places, mask: (places[0], 0)),
                pl.BlockSpec((half, columns), lambda g, places, mask: (places[1], 0)),
            ],
            out_specs=[pl.BlockSpec((half, columns), lambda g, places, mask: (0, 0))] * 2,
        ),
        out_shape=[jax.ShapeDtypeStruct((half, columns), mat_b.dtype)] * 2,
        compiler_params=pltpu.CompilerParams(vmem_limit_bytes=60 * MIB),
        name="pick_b",
    )(places, mask_b.T, mat_b, mat_b)


def mask_rows(mask_ref, a_ref, held, first_block):
    for r in range(a_ref.shape[0] // BLK):
        for k in range(a_ref.shape[1] // BLK):
            rows, cols = pl.ds(r * BLK, BLK), pl.ds(k * BLK, BLK)
            held[rows, cols] = masked(a_ref[rows, cols], mask_ref[k, first_block + r])


def own_kernel(mask_a_ref, mask_b_ref, a_ref, b_ref, out_ref, held_a, held_b):
    step = pl.program_id(0)

    @pl.when(step == 0)
    def _():
        for k in range(b_ref.shape[0] // BLK):
            for c in range(b_ref.shape[1] // BLK):
                rows, cols = pl.ds(k * BLK, BLK), pl.ds(c * BLK, BLK)
                held_b[rows, cols] = masked(b_ref[rows, cols], mask_b_ref[c, k])

    mask_rows(mask_a_ref, a_ref, held_a, step * STEP_BLOCKS)
    out_ref[...] = jnp.dot(held_a[...], held_b[...], preferred_element_type=jnp.float32)


def own_product(mat_a, mat_b, mask_a, mask_b):
    rows, depth = mat_a.shape
    columns = mat_b.shape[1]
    height = STEP_BLOCKS * BLK
    return pl.pallas_call(
        own_kernel,
        grid_spec=pltpu.PrefetchScalarGridSpec(
            num_scalar_prefetch=2,
            grid=(rows // height,),
            in_specs=[
                pl.BlockSpec((height, depth), lambda g, ma, mb: (g, 0)),
                pl.BlockSpec((depth, columns), lambda g, ma, mb: (0, 0)),
            ],
            out_specs=[
                pl.BlockSpec((height, columns), lambda g, ma, mb: (g, 0)),
                pl.BlockSpec((height, depth), lambda g, ma, mb: (g, 0)),
            ],
            scratch_shapes=[pltpu.VMEM((depth, columns), mat_b.dtype)],
        ),
        out_shape=[
            jax.ShapeDtypeStruct((rows, columns), jnp.float32),
            jax.ShapeDtypeStruct((rows, depth), mat_a.dtype),
        ],
        compiler_params=pltpu.CompilerParams(vmem_limit_bytes=24 * MIB),
        cost_estimate=pl.CostEstimate(
            flops=2 * rows * depth * columns, bytes_accessed=4 * rows * depth + 4 * rows * columns, transcendentals=0
        ),
        name="own_product",
    )(mask_a.T, mask_b.T, mat_a, mat_b)


def away_kernel(core_ref, a_ref, once_ref, twice_ref, relayed_ref, out_ref):
    rows, columns = a_ref.shape[0], out_ref.shape[1]
    half = once_ref.shape[0]
    height = STEP_BLOCKS * BLK

    def multiply(top_ref, bottom_ref):
        powers = []
        for first in range(0, rows, height):
            here = slice(first, first + height)
            product = jnp.dot(a_ref[here, :half], top_ref[...], preferred_element_type=jnp.float32)
            product += jnp.dot(a_ref[here, half:], bottom_ref[...], preferred_element_type=jnp.float32)
            pieces = product.reshape(STEP_BLOCKS, BLK, columns)
            most = jnp.max(jnp.max(jnp.abs(pieces), axis=1), axis=1, keepdims=True)
            power = jnp.ceil(jnp.log2(jnp.maximum(most, 1e-30)) + 0.01)
            scale = 32767.0 * jnp.exp2(-power)
            coded = jnp.round(pieces * scale[:, :, None])
            coded = jnp.clip(coded, -32767.0, 32767.0).reshape(height, columns)
            out_ref[here] = coded.astype(jnp.int32).astype(jnp.int16)
            powers.append(jnp.broadcast_to(power, (STEP_BLOCKS, columns)))
        powers.append(jnp.zeros((PAD - rows // BLK, columns), jnp.float32))
        out_ref[rows:] = jnp.concatenate(powers, axis=0).astype(jnp.int32).astype(jnp.int16)

    @pl.when(core_ref[0] == 0)
    def _():
        multiply(relayed_ref, twice_ref)

    @pl.when(core_ref[0] == 1)
    def _():
        multiply(twice_ref, once_ref)


def away_product(held_a, rights, core, part):
    rows, depth = held_a.shape[0] // PARTS, held_a.shape[1]
    columns = rights[0].shape[1]
    return pl.pallas_call(
        away_kernel,
        grid=(1,),
        in_specs=[pl.BlockSpec(memory_space=pltpu.SMEM), pl.BlockSpec((rows, depth), lambda g: (part, 0))]
        + [pl.BlockSpec(memory_space=pltpu.VMEM)] * len(rights),
        out_specs=pl.BlockSpec((rows + PAD, columns), lambda g: (0, 0)),
        out_shape=jax.ShapeDtypeStruct((rows + PAD, columns), jnp.int16),
        compiler_params=pltpu.CompilerParams(vmem_limit_bytes=24 * MIB),
        cost_estimate=pl.CostEstimate(
            flops=2 * rows * depth * columns, bytes_accessed=2 * rows * depth, transcendentals=0
        ),
        name="away_product",
    )(core, held_a, *rights)


def join_kernel(own_ref, coded_ref, *rest):
    out_ref, scales = rest[-2:]
    rows = coded_ref.shape[0] - PAD
    scales[...] = jnp.exp2(coded_ref[rows:].astype(jnp.int32).astype(jnp.float32)) * (1.0 / 32767.0)
    first = pl.program_id(0) * JOIN_BLOCKS
    for r in range(JOIN_BLOCKS):
        here = slice(r * BLK, (r + 1) * BLK)
        scale = scales[pl.ds(first + r, 1)]
        far = coded_ref[pl.ds(pl.multiple_of((first + r) * BLK, BLK), BLK)].astype(jnp.int32).astype(jnp.float32) * scale
        out_ref[here] = (own_ref[here] + far).astype(jnp.bfloat16)


def join(own, coded, held, part):
    columns = own.shape[1]
    height = JOIN_BLOCKS * BLK
    steps = own.shape[0] // PARTS // height
    specs = [
        pl.BlockSpec((height, columns), lambda g: (part * steps + g, 0)),
        pl.BlockSpec(memory_space=pltpu.VMEM),
    ]
    operands = [own, coded]
    aliases = {}
    if held is not None:
        specs.append(pl.BlockSpec(memory_space=pl.ANY))
        operands.append(held)
        aliases = {2: 0}
    return pl.pallas_call(
        join_kernel,
        grid=(steps,),
        in_specs=specs,
        out_specs=pl.BlockSpec((height, columns), lambda g: (part * steps + g, 0)),
        out_shape=jax.ShapeDtypeStruct(own.shape, jnp.bfloat16),
        scratch_shapes=[pltpu.VMEM((PAD, columns), jnp.float32)],
        input_output_aliases=aliases,
        compiler_params=pltpu.CompilerParams(vmem_limit_bytes=24 * MIB),
        cost_estimate=pl.CostEstimate(
            flops=2 * steps * height * columns, bytes_accessed=8 * steps * height * columns, transcendentals=0
        ),
        name="join",
    )(*operands)


def routes(n_row, n_col):
    def place(device):
        i, j = divmod(device, n_col)
        return j // 2, (j % 2) * (n_row // 2) + i // 2, i % 2

    def at(plane, z, core):
        half, low = divmod(z % n_row, n_row // 2)
        return (low * 2 + core) * n_col + plane * 2 + half

    devices = range(n_row * n_col)
    give_b = [(d, ((d // n_col - 1) % n_row) * n_col + (d % n_col + 1) % n_col) for d in devices]
    give_c = [(d, d // n_col * n_col + (d % n_col - 1) % n_col) for d in devices]
    first_leg, second_leg = [], []
    for source, target in give_b:
        plane, z, core = place(target)
        if core == 1:
            first_leg.append((source, target))
        else:
            middle = at(plane, z + 2, core)
            first_leg.append((source, middle))
            second_leg.append((middle, target))
    return give_b, first_leg, second_leg, give_c


def body(mat_a, mat_b, mask_a, mask_b):
    depth = mat_a.shape[1]
    axes = ("row", "col")
    give_b, first_leg, second_leg, give_c = routes(lax.axis_size("row"), lax.axis_size("col"))
    place = lax.axis_index("row")
    slot = jnp.where(place == 0, 1, 0).astype(jnp.int32)
    core = lax.rem(place, 2).astype(jnp.int32)
    places = jnp.stack([2 * slot + 1 - core, 2 * slot + core])
    once, twice = pick_b(mat_b, mask_b, places, depth // 2)
    once = lax.ppermute(once, axes, first_leg)
    twice = lax.ppermute(twice, axes, give_b)
    relayed = lax.ppermute(once, axes, second_leg)
    own, held_a = own_product(mat_a, mat_b, mask_a, mask_b)
    arrived = []
    for part in range(PARTS):
        coded = away_product(held_a, [once, twice, relayed], core[None], part)
        arrived.append(lax.ppermute(coded, axes, give_c))
    out = None
    for part in range(PARTS):
        out = join(own, arrived[part], out, part)
    return out


def solution(mesh):
    return jax.shard_map(
        body,
        mesh=mesh,
        in_specs=(P("row", "col"), P("row", "col"), P("row", "col"), P("row", "col")),
        out_specs=P("row", "col"),
        check_vma=False,
    )
```

```python
import functools

import jax
import jax.numpy as jnp
from jax import lax
from jax.experimental import pallas as pl
from jax.experimental.pallas import tpu as pltpu
from jax.sharding import PartitionSpec as P

BLK = 128
STEP_BLOCKS = 5
PAD = 16
JOIN_BLOCKS = 5
PARTS = 2
MIB = 1024 * 1024


def masked(block, flag):
    return jnp.where(flag > 0, block, jnp.zeros_like(block))


def place_of(row, which):
    slot = jnp.where(row == 0, 1, 0)
    core = lax.rem(row, 2)
    return 2 * slot + (1 - core if which == 0 else core)


def pick_b(mat_b, mask_b, row, which, half):
    columns = mat_b.shape[1]
    blocks = half // BLK
    place = place_of(row, which)
    piece = lax.dynamic_slice_in_dim(mat_b, place * half, half, 0)
    flags = lax.dynamic_slice_in_dim(mask_b, place * blocks, blocks, 0)
    kept = piece.reshape(blocks, BLK, columns // BLK, BLK) * flags.astype(mat_b.dtype)[:, None, :, None]
    return kept.reshape(half, columns)


def mask_rows(mask_ref, a_ref, held, first_block):
    for r in range(a_ref.shape[0] // BLK):
        for k in range(a_ref.shape[1] // BLK):
            rows, cols = pl.ds(r * BLK, BLK), pl.ds(k * BLK, BLK)
            held[rows, cols] = masked(a_ref[rows, cols], mask_ref[k, first_block + r])


def own_kernel(mask_a_ref, mask_b_ref, a_ref, b_ref, out_ref, held_a, done_ref, held_b):
    step = pl.program_id(0)
    done_ref[...] = jnp.zeros_like(done_ref)

    @pl.when(step == 0)
    def _():
        for k in range(b_ref.shape[0] // BLK):
            for c in range(b_ref.shape[1] // BLK):
                rows, cols = pl.ds(k * BLK, BLK), pl.ds(c * BLK, BLK)
                held_b[rows, cols] = masked(b_ref[rows, cols], mask_b_ref[c, k])

    mask_rows(mask_a_ref, a_ref, held_a, step * STEP_BLOCKS)
    out_ref[...] = jnp.dot(held_a[...], held_b[...], preferred_element_type=jnp.float32)


def own_product(mat_a, mat_b, mask_a, mask_b):
    rows, depth = mat_a.shape
    columns = mat_b.shape[1]
    height = STEP_BLOCKS * BLK
    return pl.pallas_call(
        own_kernel,
        grid_spec=pltpu.PrefetchScalarGridSpec(
            num_scalar_prefetch=2,
            grid=(rows // height,),
            in_specs=[
                pl.BlockSpec((height, depth), lambda g, ma, mb: (g, 0)),
                pl.BlockSpec((depth, columns), lambda g, ma, mb: (0, 0)),
            ],
            out_specs=[
                pl.BlockSpec((height, columns), lambda g, ma, mb: (g, 0)),
                pl.BlockSpec((height, depth), lambda g, ma, mb: (g, 0)),
                pl.BlockSpec((8, BLK), lambda g, ma, mb: (0, 0)),
            ],
            scratch_shapes=[pltpu.VMEM((depth, columns), mat_b.dtype)],
        ),
        out_shape=[
            jax.ShapeDtypeStruct((rows, columns), jnp.float32),
            jax.ShapeDtypeStruct((rows, depth), mat_a.dtype),
            jax.ShapeDtypeStruct((8, BLK), jnp.float32),
        ],
        compiler_params=pltpu.CompilerParams(vmem_limit_bytes=24 * MIB),
        cost_estimate=pl.CostEstimate(
            flops=2 * rows * depth * columns, bytes_accessed=4 * rows * depth + 4 * rows * columns, transcendentals=0
        ),
        name="own_product",
    )(mask_a.T, mask_b.T, mat_a, mat_b)


def after_kernel(value_ref, done_ref, out_ref):
    pass


def after(value, done):
    return pl.pallas_call(
        after_kernel,
        in_specs=[pl.BlockSpec(memory_space=pl.ANY)] * 2,
        out_specs=pl.BlockSpec(memory_space=pl.ANY),
        out_shape=jax.ShapeDtypeStruct(value.shape, value.dtype),
        input_output_aliases={0: 0},
        compiler_params=pltpu.CompilerParams(vmem_limit_bytes=MIB),
        name="after",
    )(value, done)


def away_kernel(core_ref, a_ref, once_ref, twice_ref, relayed_ref, out_ref):
    rows, columns = a_ref.shape[0], out_ref.shape[1]
    half = once_ref.shape[0]
    height = STEP_BLOCKS * BLK

    def multiply(top_ref, bottom_ref):
        powers = []
        for first in range(0, rows, height):
            here = slice(first, first + height)
            product = jnp.dot(a_ref[here, :half], top_ref[...], preferred_element_type=jnp.float32)
            product += jnp.dot(a_ref[here, half:], bottom_ref[...], preferred_element_type=jnp.float32)
            pieces = product.reshape(STEP_BLOCKS, BLK, columns)
            most = jnp.max(jnp.max(jnp.abs(pieces), axis=1), axis=1, keepdims=True)
            power = jnp.ceil(jnp.log2(jnp.maximum(most, 1e-30)) + 0.01)
            scale = 32767.0 * jnp.exp2(-power)
            coded = jnp.round(pieces * scale[:, :, None])
            coded = jnp.clip(coded, -32767.0, 32767.0).reshape(height, columns)
            out_ref[here] = coded.astype(jnp.int32).astype(jnp.int16)
            powers.append(jnp.broadcast_to(power, (STEP_BLOCKS, columns)))
        powers.append(jnp.zeros((PAD - rows // BLK, columns), jnp.float32))
        out_ref[rows:] = jnp.concatenate(powers, axis=0).astype(jnp.int32).astype(jnp.int16)

    @pl.when(core_ref[0] == 0)
    def _():
        multiply(relayed_ref, twice_ref)

    @pl.when(core_ref[0] == 1)
    def _():
        multiply(twice_ref, once_ref)


def away_product(held_a, rights, core, part):
    rows, depth = held_a.shape[0] // PARTS, held_a.shape[1]
    columns = rights[0].shape[1]
    return pl.pallas_call(
        away_kernel,
        grid=(1,),
        in_specs=[pl.BlockSpec(memory_space=pltpu.SMEM), pl.BlockSpec((rows, depth), lambda g: (part, 0))]
        + [pl.BlockSpec(memory_space=pltpu.VMEM)] * len(rights),
        out_specs=pl.BlockSpec((rows + PAD, columns), lambda g: (0, 0)),
        out_shape=jax.ShapeDtypeStruct((rows + PAD, columns), jnp.int16),
        compiler_params=pltpu.CompilerParams(vmem_limit_bytes=24 * MIB),
        cost_estimate=pl.CostEstimate(
            flops=2 * rows * depth * columns, bytes_accessed=2 * rows * depth, transcendentals=0
        ),
        name="away_product",
    )(core, held_a, *rights)


def join_kernel(own_ref, coded_ref, *rest, start):
    out_ref, scales = rest[-2:]
    rows = coded_ref.shape[0] - PAD
    scales[...] = jnp.exp2(coded_ref[rows:].astype(jnp.int32).astype(jnp.float32)) * (1.0 / 32767.0)
    first = pl.program_id(0) * JOIN_BLOCKS
    for r in range(JOIN_BLOCKS):
        here = slice(r * BLK, (r + 1) * BLK)
        there = pl.ds(pl.multiple_of((start + first + r) * BLK, BLK), BLK)
        scale = scales[pl.ds(first + r, 1)]
        far = coded_ref[pl.ds(pl.multiple_of((first + r) * BLK, BLK), BLK)].astype(jnp.int32).astype(jnp.float32) * scale
        out_ref[here] = (own_ref[there] + far).astype(jnp.bfloat16)


def join(own, coded, held, part):
    columns = own.shape[1]
    height = JOIN_BLOCKS * BLK
    steps = own.shape[0] // PARTS // height
    specs = [
        pl.BlockSpec(memory_space=pltpu.VMEM),
        pl.BlockSpec(memory_space=pltpu.VMEM),
    ]
    operands = [own, coded]
    aliases = {}
    if held is not None:
        specs.append(pl.BlockSpec(memory_space=pl.ANY))
        operands.append(held)
        aliases = {2: 0}
    return pl.pallas_call(
        functools.partial(join_kernel, start=part * steps * JOIN_BLOCKS),
        grid=(steps,),
        in_specs=specs,
        out_specs=pl.BlockSpec((height, columns), lambda g: (part * steps + g, 0)),
        out_shape=jax.ShapeDtypeStruct(own.shape, jnp.bfloat16),
        scratch_shapes=[pltpu.VMEM((PAD, columns), jnp.float32)],
        input_output_aliases=aliases,
        compiler_params=pltpu.CompilerParams(vmem_limit_bytes=24 * MIB),
        cost_estimate=pl.CostEstimate(
            flops=2 * steps * height * columns, bytes_accessed=8 * steps * height * columns, transcendentals=0
        ),
        name="join",
    )(*operands)


def routes(n_row, n_col):
    def place(device):
        i, j = divmod(device, n_col)
        return j // 2, (j % 2) * (n_row // 2) + i // 2, i % 2

    def at(plane, z, core):
        half, low = divmod(z % n_row, n_row // 2)
        return (low * 2 + core) * n_col + plane * 2 + half

    devices = range(n_row * n_col)
    give_b = [(d, ((d // n_col - 1) % n_row) * n_col + (d % n_col + 1) % n_col) for d in devices]
    give_c = [(d, d // n_col * n_col + (d % n_col - 1) % n_col) for d in devices]
    first_leg, second_leg = [], []
    for source, target in give_b:
        plane, z, core = place(target)
        if core == 1:
            first_leg.append((source, target))
        else:
            middle = at(plane, z + 2, core)
            first_leg.append((source, middle))
            second_leg.append((middle, target))
    return give_b, first_leg, second_leg, give_c


def body(mat_a, mat_b, mask_a, mask_b):
    depth = mat_a.shape[1]
    axes = ("row", "col")
    give_b, first_leg, second_leg, give_c = routes(lax.axis_size("row"), lax.axis_size("col"))
    place = lax.axis_index("row").astype(jnp.int32)
    core = lax.rem(place, 2)
    once = lax.ppermute(pick_b(mat_b, mask_b, place, 0, depth // 2), axes, first_leg)
    twice = lax.ppermute(pick_b(mat_b, mask_b, place, 1, depth // 2), axes, give_b)
    own, held_a, done = own_product(mat_a, mat_b, mask_a, mask_b)
    once = after(once, done)
    relayed = lax.ppermute(once, axes, second_leg)
    arrived = []
    for part in range(PARTS):
        coded = away_product(held_a, [once, twice, relayed], core[None], part)
        arrived.append(lax.ppermute(coded, axes, give_c))
    out = None
    for part in range(PARTS):
        out = join(own, arrived[part], out, part)
    return out


def solution(mesh):
    return jax.shard_map(
        body,
        mesh=mesh,
        in_specs=(P("row", "col"), P("row", "col"), P("row", "col"), P("row", "col")),
        out_specs=P("row", "col"),
        check_vma=False,
    )
```

```python
import functools

import jax
import jax.numpy as jnp
from jax import lax
from jax.experimental import pallas as pl
from jax.experimental.pallas import tpu as pltpu
from jax.sharding import PartitionSpec as P

BLK = 128
STEP_BLOCKS = 5
PAD = 16
JOIN_BLOCKS = 5
PARTS = 2
MIB = 1024 * 1024


def masked(block, flag):
    return jnp.where(flag > 0, block, jnp.zeros_like(block))


def place_of(row, which):
    slot = jnp.where(row == 0, 1, 0)
    core = lax.rem(row, 2)
    return 2 * slot + (1 - core if which == 0 else core)


def pick_b(mat_b, mask_b, row, which, half):
    columns = mat_b.shape[1]
    blocks = half // BLK
    place = place_of(row, which)
    piece = lax.dynamic_slice_in_dim(mat_b, place * half, half, 0)
    flags = lax.dynamic_slice_in_dim(mask_b, place * blocks, blocks, 0)
    kept = jnp.repeat(jnp.repeat(flags > 0, BLK, 1), BLK, 0)
    return jnp.where(kept, piece, jnp.zeros_like(piece))


def mask_rows(mask_ref, a_ref, held, first_block):
    for r in range(a_ref.shape[0] // BLK):
        for k in range(a_ref.shape[1] // BLK):
            rows, cols = pl.ds(r * BLK, BLK), pl.ds(k * BLK, BLK)
            held[rows, cols] = masked(a_ref[rows, cols], mask_ref[k, first_block + r])


def own_kernel(mask_a_ref, mask_b_ref, a_ref, b_ref, out_ref, held_a, done_ref, held_b):
    step = pl.program_id(0)
    done_ref[...] = jnp.zeros_like(done_ref)

    @pl.when(step == 0)
    def _():
        for k in range(b_ref.shape[0] // BLK):
            for c in range(b_ref.shape[1] // BLK):
                rows, cols = pl.ds(k * BLK, BLK), pl.ds(c * BLK, BLK)
                held_b[rows, cols] = masked(b_ref[rows, cols], mask_b_ref[c, k])

    mask_rows(mask_a_ref, a_ref, held_a, step * STEP_BLOCKS)
    out_ref[...] = jnp.dot(held_a[...], held_b[...], preferred_element_type=jnp.float32)


def own_product(mat_a, mat_b, mask_a, mask_b):
    rows, depth = mat_a.shape
    columns = mat_b.shape[1]
    height = STEP_BLOCKS * BLK
    return pl.pallas_call(
        own_kernel,
        grid_spec=pltpu.PrefetchScalarGridSpec(
            num_scalar_prefetch=2,
            grid=(rows // height,),
            in_specs=[
                pl.BlockSpec((height, depth), lambda g, ma, mb: (g, 0)),
                pl.BlockSpec((depth, columns), lambda g, ma, mb: (0, 0)),
            ],
            out_specs=[
                pl.BlockSpec((height, columns), lambda g, ma, mb: (g, 0)),
                pl.BlockSpec((height, depth), lambda g, ma, mb: (g, 0)),
                pl.BlockSpec((8, BLK), lambda g, ma, mb: (0, 0)),
            ],
            scratch_shapes=[pltpu.VMEM((depth, columns), mat_b.dtype)],
        ),
        out_shape=[
            jax.ShapeDtypeStruct((rows, columns), jnp.float32),
            jax.ShapeDtypeStruct((rows, depth), mat_a.dtype),
            jax.ShapeDtypeStruct((8, BLK), jnp.float32),
        ],
        compiler_params=pltpu.CompilerParams(vmem_limit_bytes=24 * MIB),
        cost_estimate=pl.CostEstimate(
            flops=2 * rows * depth * columns, bytes_accessed=4 * rows * depth + 4 * rows * columns, transcendentals=0
        ),
        name="own_product",
    )(mask_a.T, mask_b.T, mat_a, mat_b)


def after_kernel(value_ref, done_ref, out_ref):
    pass


def after(value, done):
    return pl.pallas_call(
        after_kernel,
        in_specs=[pl.BlockSpec(memory_space=pl.ANY)] * 2,
        out_specs=pl.BlockSpec(memory_space=pl.ANY),
        out_shape=jax.ShapeDtypeStruct(value.shape, value.dtype),
        input_output_aliases={0: 0},
        compiler_params=pltpu.CompilerParams(vmem_limit_bytes=MIB),
        name="after",
    )(value, done)


def away_kernel(core_ref, a_ref, once_ref, twice_ref, relayed_ref, out_ref):
    rows, columns = a_ref.shape[0], out_ref.shape[1]
    half = once_ref.shape[0]
    height = STEP_BLOCKS * BLK

    def multiply(top_ref, bottom_ref):
        powers = []
        for first in range(0, rows, height):
            here = slice(first, first + height)
            product = jnp.dot(a_ref[here, :half], top_ref[...], preferred_element_type=jnp.float32)
            product += jnp.dot(a_ref[here, half:], bottom_ref[...], preferred_element_type=jnp.float32)
            pieces = product.reshape(STEP_BLOCKS, BLK, columns)
            most = jnp.max(jnp.max(jnp.abs(pieces), axis=1), axis=1, keepdims=True)
            power = jnp.ceil(jnp.log2(jnp.maximum(most, 1e-30)) + 0.01)
            scale = 32767.0 * jnp.exp2(-power)
            coded = jnp.round(pieces * scale[:, :, None])
            coded = jnp.clip(coded, -32767.0, 32767.0).reshape(height, columns)
            out_ref[here] = coded.astype(jnp.int32).astype(jnp.int16)
            powers.append(jnp.broadcast_to(power, (STEP_BLOCKS, columns)))
        powers.append(jnp.zeros((PAD - rows // BLK, columns), jnp.float32))
        out_ref[rows:] = jnp.concatenate(powers, axis=0).astype(jnp.int32).astype(jnp.int16)

    @pl.when(core_ref[0] == 0)
    def _():
        multiply(relayed_ref, twice_ref)

    @pl.when(core_ref[0] == 1)
    def _():
        multiply(twice_ref, once_ref)


def away_product(held_a, rights, core, part):
    rows, depth = held_a.shape[0] // PARTS, held_a.shape[1]
    columns = rights[0].shape[1]
    return pl.pallas_call(
        away_kernel,
        grid=(1,),
        in_specs=[pl.BlockSpec(memory_space=pltpu.SMEM), pl.BlockSpec((rows, depth), lambda g: (part, 0))]
        + [pl.BlockSpec(memory_space=pltpu.VMEM)] * len(rights),
        out_specs=pl.BlockSpec((rows + PAD, columns), lambda g: (0, 0)),
        out_shape=jax.ShapeDtypeStruct((rows + PAD, columns), jnp.int16),
        compiler_params=pltpu.CompilerParams(vmem_limit_bytes=24 * MIB),
        cost_estimate=pl.CostEstimate(
            flops=2 * rows * depth * columns, bytes_accessed=2 * rows * depth, transcendentals=0
        ),
        name="away_product",
    )(core, held_a, *rights)


def join_kernel(own_ref, coded_ref, *rest, start):
    out_ref, scales = rest[-2:]
    rows = coded_ref.shape[0] - PAD
    scales[...] = jnp.exp2(coded_ref[rows:].astype(jnp.int32).astype(jnp.float32)) * (1.0 / 32767.0)
    first = pl.program_id(0) * JOIN_BLOCKS
    for r in range(JOIN_BLOCKS):
        here = slice(r * BLK, (r + 1) * BLK)
        there = pl.ds(pl.multiple_of((start + first + r) * BLK, BLK), BLK)
        scale = scales[pl.ds(first + r, 1)]
        far = coded_ref[pl.ds(pl.multiple_of((first + r) * BLK, BLK), BLK)].astype(jnp.int32).astype(jnp.float32) * scale
        out_ref[here] = (own_ref[there] + far).astype(jnp.bfloat16)


def join(own, coded, held, part):
    columns = own.shape[1]
    height = JOIN_BLOCKS * BLK
    steps = own.shape[0] // PARTS // height
    specs = [
        pl.BlockSpec(memory_space=pltpu.VMEM),
        pl.BlockSpec(memory_space=pltpu.VMEM),
    ]
    operands = [own, coded]
    aliases = {}
    if held is not None:
        specs.append(pl.BlockSpec(memory_space=pl.ANY))
        operands.append(held)
        aliases = {2: 0}
    return pl.pallas_call(
        functools.partial(join_kernel, start=part * steps * JOIN_BLOCKS),
        grid=(steps,),
        in_specs=specs,
        out_specs=pl.BlockSpec((height, columns), lambda g: (part * steps + g, 0)),
        out_shape=jax.ShapeDtypeStruct(own.shape, jnp.bfloat16),
        scratch_shapes=[pltpu.VMEM((PAD, columns), jnp.float32)],
        input_output_aliases=aliases,
        compiler_params=pltpu.CompilerParams(vmem_limit_bytes=24 * MIB),
        cost_estimate=pl.CostEstimate(
            flops=2 * steps * height * columns, bytes_accessed=8 * steps * height * columns, transcendentals=0
        ),
        name="join",
    )(*operands)


def routes(n_row, n_col):
    def place(device):
        i, j = divmod(device, n_col)
        return j // 2, (j % 2) * (n_row // 2) + i // 2, i % 2

    def at(plane, z, core):
        half, low = divmod(z % n_row, n_row // 2)
        return (low * 2 + core) * n_col + plane * 2 + half

    devices = range(n_row * n_col)
    give_b = [(d, ((d // n_col - 1) % n_row) * n_col + (d % n_col + 1) % n_col) for d in devices]
    give_c = [(d, d // n_col * n_col + (d % n_col - 1) % n_col) for d in devices]
    first_leg, second_leg = [], []
    for source, target in give_b:
        plane, z, core = place(target)
        if core == 1:
            first_leg.append((source, target))
        else:
            middle = at(plane, z + 2, core)
            first_leg.append((source, middle))
            second_leg.append((middle, target))
    return give_b, first_leg, second_leg, give_c


def body(mat_a, mat_b, mask_a, mask_b):
    depth = mat_a.shape[1]
    axes = ("row", "col")
    give_b, first_leg, second_leg, give_c = routes(lax.axis_size("row"), lax.axis_size("col"))
    place = lax.axis_index("row").astype(jnp.int32)
    core = lax.rem(place, 2)
    once = lax.ppermute(pick_b(mat_b, mask_b, place, 0, depth // 2), axes, first_leg)
    twice = lax.ppermute(pick_b(mat_b, mask_b, place, 1, depth // 2), axes, give_b)
    own, held_a, done = own_product(mat_a, mat_b, mask_a, mask_b)
    once = after(once, done)
    relayed = lax.ppermute(once, axes, second_leg)
    arrived = []
    for part in range(PARTS):
        coded = away_product(held_a, [once, twice, relayed], core[None], part)
        arrived.append(lax.ppermute(coded, axes, give_c))
    out = None
    for part in range(PARTS):
        out = join(own, arrived[part], out, part)
    return out


def solution(mesh):
    return jax.shard_map(
        body,
        mesh=mesh,
        in_specs=(P("row", "col"), P("row", "col"), P("row", "col"), P("row", "col")),
        out_specs=P("row", "col"),
        check_vma=False,
    )
```

```python
import functools

import jax
import jax.numpy as jnp
from jax import lax
from jax.experimental import pallas as pl
from jax.experimental.pallas import tpu as pltpu
from jax.sharding import PartitionSpec as P

BLK = 128
STEP_BLOCKS = 5
PAD = 16
JOIN_BLOCKS = 5
PARTS = 4
MIB = 1024 * 1024


def masked(block, flag):
    return jnp.where(flag > 0, block, jnp.zeros_like(block))


def place_of(row, which):
    slot = jnp.where(row == 0, 1, 0)
    core = lax.rem(row, 2)
    return 2 * slot + (1 - core if which == 0 else core)


def pick_b(mat_b, mask_b, row, which, half):
    columns = mat_b.shape[1]
    blocks = half // BLK
    place = place_of(row, which)
    piece = lax.dynamic_slice_in_dim(mat_b, place * half, half, 0)
    flags = lax.dynamic_slice_in_dim(mask_b, place * blocks, blocks, 0)
    kept = jnp.repeat(jnp.repeat(flags > 0, BLK, 1), BLK, 0)
    return jnp.where(kept, piece, jnp.zeros_like(piece))


def mask_rows(mask_ref, a_ref, held, first_block):
    for r in range(a_ref.shape[0] // BLK):
        for k in range(a_ref.shape[1] // BLK):
            rows, cols = pl.ds(r * BLK, BLK), pl.ds(k * BLK, BLK)
            held[rows, cols] = masked(a_ref[rows, cols], mask_ref[k, first_block + r])


def own_kernel(mask_a_ref, mask_b_ref, a_ref, b_ref, out_ref, held_a, done_ref, held_b):
    step = pl.program_id(0)
    done_ref[...] = jnp.zeros_like(done_ref)

    @pl.when(step == 0)
    def _():
        for k in range(b_ref.shape[0] // BLK):
            for c in range(b_ref.shape[1] // BLK):
                rows, cols = pl.ds(k * BLK, BLK), pl.ds(c * BLK, BLK)
                held_b[rows, cols] = masked(b_ref[rows, cols], mask_b_ref[c, k])

    mask_rows(mask_a_ref, a_ref, held_a, step * STEP_BLOCKS)
    out_ref[...] = jnp.dot(held_a[...], held_b[...], preferred_element_type=jnp.float32)


def own_product(mat_a, mat_b, mask_a, mask_b):
    rows, depth = mat_a.shape
    columns = mat_b.shape[1]
    height = STEP_BLOCKS * BLK
    return pl.pallas_call(
        own_kernel,
        grid_spec=pltpu.PrefetchScalarGridSpec(
            num_scalar_prefetch=2,
            grid=(rows // height,),
            in_specs=[
                pl.BlockSpec((height, depth), lambda g, ma, mb: (g, 0)),
                pl.BlockSpec((depth, columns), lambda g, ma, mb: (0, 0)),
            ],
            out_specs=[
                pl.BlockSpec((height, columns), lambda g, ma, mb: (g, 0)),
                pl.BlockSpec((height, depth), lambda g, ma, mb: (g, 0)),
                pl.BlockSpec((8, BLK), lambda g, ma, mb: (0, 0)),
            ],
            scratch_shapes=[pltpu.VMEM((depth, columns), mat_b.dtype)],
        ),
        out_shape=[
            jax.ShapeDtypeStruct((rows, columns), jnp.float32),
            jax.ShapeDtypeStruct((rows, depth), mat_a.dtype),
            jax.ShapeDtypeStruct((8, BLK), jnp.float32),
        ],
        compiler_params=pltpu.CompilerParams(vmem_limit_bytes=24 * MIB),
        cost_estimate=pl.CostEstimate(
            flops=2 * rows * depth * columns, bytes_accessed=4 * rows * depth + 4 * rows * columns, transcendentals=0
        ),
        name="own_product",
    )(mask_a.T, mask_b.T, mat_a, mat_b)


def after_kernel(value_ref, done_ref, out_ref):
    pass


def after(value, done):
    return pl.pallas_call(
        after_kernel,
        in_specs=[pl.BlockSpec(memory_space=pl.ANY)] * 2,
        out_specs=pl.BlockSpec(memory_space=pl.ANY),
        out_shape=jax.ShapeDtypeStruct(value.shape, value.dtype),
        input_output_aliases={0: 0},
        compiler_params=pltpu.CompilerParams(vmem_limit_bytes=MIB),
        name="after",
    )(value, done)


def away_kernel(core_ref, a_ref, once_ref, twice_ref, relayed_ref, out_ref):
    rows, columns = a_ref.shape[0], out_ref.shape[1]
    half = once_ref.shape[0]
    height = STEP_BLOCKS * BLK

    def multiply(top_ref, bottom_ref):
        powers = []
        for first in range(0, rows, height):
            here = slice(first, first + height)
            product = jnp.dot(a_ref[here, :half], top_ref[...], preferred_element_type=jnp.float32)
            product += jnp.dot(a_ref[here, half:], bottom_ref[...], preferred_element_type=jnp.float32)
            pieces = product.reshape(STEP_BLOCKS, BLK, columns)
            most = jnp.max(jnp.max(jnp.abs(pieces), axis=1), axis=1, keepdims=True)
            power = jnp.ceil(jnp.log2(jnp.maximum(most, 1e-30)) + 0.01)
            scale = 32767.0 * jnp.exp2(-power)
            coded = jnp.round(pieces * scale[:, :, None])
            coded = jnp.clip(coded, -32767.0, 32767.0).reshape(height, columns)
            out_ref[here] = coded.astype(jnp.int32).astype(jnp.int16)
            powers.append(jnp.broadcast_to(power, (STEP_BLOCKS, columns)))
        powers.append(jnp.zeros((PAD - rows // BLK, columns), jnp.float32))
        out_ref[rows:] = jnp.concatenate(powers, axis=0).astype(jnp.int32).astype(jnp.int16)

    @pl.when(core_ref[0] == 0)
    def _():
        multiply(relayed_ref, twice_ref)

    @pl.when(core_ref[0] == 1)
    def _():
        multiply(twice_ref, once_ref)


def away_product(held_a, rights, core, part):
    rows, depth = held_a.shape[0] // PARTS, held_a.shape[1]
    columns = rights[0].shape[1]
    return pl.pallas_call(
        away_kernel,
        grid=(1,),
        in_specs=[pl.BlockSpec(memory_space=pltpu.SMEM), pl.BlockSpec((rows, depth), lambda g: (part, 0))]
        + [pl.BlockSpec(memory_space=pltpu.VMEM)] * len(rights),
        out_specs=pl.BlockSpec((rows + PAD, columns), lambda g: (0, 0)),
        out_shape=jax.ShapeDtypeStruct((rows + PAD, columns), jnp.int16),
        compiler_params=pltpu.CompilerParams(vmem_limit_bytes=24 * MIB),
        cost_estimate=pl.CostEstimate(
            flops=2 * rows * depth * columns, bytes_accessed=2 * rows * depth, transcendentals=0
        ),
        name="away_product",
    )(core, held_a, *rights)


def join_kernel(own_ref, coded_ref, *rest, start):
    out_ref, scales = rest[-2:]
    rows = coded_ref.shape[0] - PAD
    scales[...] = jnp.exp2(coded_ref[rows:].astype(jnp.int32).astype(jnp.float32)) * (1.0 / 32767.0)
    first = pl.program_id(0) * JOIN_BLOCKS
    for r in range(JOIN_BLOCKS):
        here = slice(r * BLK, (r + 1) * BLK)
        there = pl.ds(pl.multiple_of((start + first + r) * BLK, BLK), BLK)
        scale = scales[pl.ds(first + r, 1)]
        far = coded_ref[pl.ds(pl.multiple_of((first + r) * BLK, BLK), BLK)].astype(jnp.int32).astype(jnp.float32) * scale
        out_ref[here] = (own_ref[there] + far).astype(jnp.bfloat16)


def join(own, coded, held, part):
    columns = own.shape[1]
    height = JOIN_BLOCKS * BLK
    steps = own.shape[0] // PARTS // height
    specs = [
        pl.BlockSpec(memory_space=pltpu.VMEM),
        pl.BlockSpec(memory_space=pltpu.VMEM),
    ]
    operands = [own, coded]
    aliases = {}
    if held is not None:
        specs.append(pl.BlockSpec(memory_space=pl.ANY))
        operands.append(held)
        aliases = {2: 0}
    return pl.pallas_call(
        functools.partial(join_kernel, start=part * steps * JOIN_BLOCKS),
        grid=(steps,),
        in_specs=specs,
        out_specs=pl.BlockSpec((height, columns), lambda g: (part * steps + g, 0)),
        out_shape=jax.ShapeDtypeStruct(own.shape, jnp.bfloat16),
        scratch_shapes=[pltpu.VMEM((PAD, columns), jnp.float32)],
        input_output_aliases=aliases,
        compiler_params=pltpu.CompilerParams(vmem_limit_bytes=24 * MIB),
        cost_estimate=pl.CostEstimate(
            flops=2 * steps * height * columns, bytes_accessed=8 * steps * height * columns, transcendentals=0
        ),
        name="join",
    )(*operands)


def routes(n_row, n_col):
    def place(device):
        i, j = divmod(device, n_col)
        return j // 2, (j % 2) * (n_row // 2) + i // 2, i % 2

    def at(plane, z, core):
        half, low = divmod(z % n_row, n_row // 2)
        return (low * 2 + core) * n_col + plane * 2 + half

    devices = range(n_row * n_col)
    give_b = [(d, ((d // n_col - 1) % n_row) * n_col + (d % n_col + 1) % n_col) for d in devices]
    give_c = [(d, d // n_col * n_col + (d % n_col - 1) % n_col) for d in devices]
    first_leg, second_leg = [], []
    for source, target in give_b:
        plane, z, core = place(target)
        if core == 1:
            first_leg.append((source, target))
        else:
            middle = at(plane, z + 2, core)
            first_leg.append((source, middle))
            second_leg.append((middle, target))
    return give_b, first_leg, second_leg, give_c


def body(mat_a, mat_b, mask_a, mask_b):
    depth = mat_a.shape[1]
    axes = ("row", "col")
    give_b, first_leg, second_leg, give_c = routes(lax.axis_size("row"), lax.axis_size("col"))
    place = lax.axis_index("row").astype(jnp.int32)
    core = lax.rem(place, 2)
    once = lax.ppermute(pick_b(mat_b, mask_b, place, 0, depth // 2), axes, first_leg)
    twice = lax.ppermute(pick_b(mat_b, mask_b, place, 1, depth // 2), axes, give_b)
    own, held_a, done = own_product(mat_a, mat_b, mask_a, mask_b)
    once = after(once, done)
    relayed = lax.ppermute(once, axes, second_leg)
    arrived = []
    for part in range(PARTS):
        coded = away_product(held_a, [once, twice, relayed], core[None], part)
        arrived.append(lax.ppermute(coded, axes, give_c))
    out = None
    for part in range(PARTS):
        out = join(own, arrived[part], out, part)
    return out


def solution(mesh):
    return jax.shard_map(
        body,
        mesh=mesh,
        in_specs=(P("row", "col"), P("row", "col"), P("row", "col"), P("row", "col")),
        out_specs=P("row", "col"),
        check_vma=False,
    )
```
